128 devices in a mesh: span: 16 (over y, z), wall: 8 (over x, core).
Axes of the slice: x: 4, y: 4, z: 4, core: 2. Of those that a mesh axis runs over, the one named last changes fastest.
Arguments:
- stress: float32 [2, 32, 1024, 2048], P(None, None, 'wall', 'span'), may hold values from -8 to 8
Outputs:
- pressure: float32 [2, 32, 1024, 2048], P(None, None, 'wall', 'span')
The draws below stay inside these ranges and needn't reach their ends.
All inputs are finite; a program needn't handle non-finite values.
Results may differ from the reference program's by a relative error of at most 0.00035.
Values sent between devices are 32-bit elements; how exact they have to be, the bound alone decides.
A program may use at most 128 MiB of HBM per device.

```python
import math
import jax
import jax.numpy as jnp
from jax import lax

NZ = 2048
NY = 1024
KX = 32


def draw_stress(key, part):
    full_shape = (2, KX, NY, NZ)
    key_rough = jax.random.fold_in(key, 0)
    key_coef = jax.random.fold_in(key, 2)
    mode_total = 8
    row_frac = (jnp.arange(NY, dtype=jnp.int32).astype(jnp.float32) + 0.5) / NY
    profiles = [jnp.sin(math.pi * row_frac), jnp.sin(2.0 * math.pi * row_frac), jnp.sin(3.0 * math.pi * row_frac)]
    cell_ids = jnp.arange(NZ, dtype=jnp.int32)
    coef_shape = (2, KX, mode_total, 2, 3)
    coefs = jax.random.normal(key_coef, coef_shape, jnp.float32)
    red_part = jnp.zeros(full_shape, jnp.float32)
    for mode_number in range(1, mode_total + 1):
        amplitude = 1.2 / (1.0 + (mode_number / 3.0) ** 2)
        phase = (mode_number * cell_ids % NZ).astype(jnp.float32) * (2.0 * math.pi / NZ)
        bases = (jnp.cos(phase), jnp.sin(phase))
        for trig_index in range(2):
            profile = jnp.zeros((2, KX, NY), jnp.float32)
            for prof_index in range(3):
                profile = profile + coefs[:, :, mode_number - 1, trig_index, prof_index][:, :, None] * profiles[prof_index][None, None, :]
            red_part = red_part + amplitude * profile[:, :, :, None] * bases[trig_index][None, None, None, :]
    total = jax.random.normal(key_rough, full_shape, jnp.float32) + red_part
    return jnp.clip(total, -8.0, 8.0)


def setup_inputs(seed: int = 0) -> dict:
    seeds = jax.random.split(jax.random.key(seed), 2)
    stress = draw_stress(jax.random.fold_in(seeds[1], 71), 0)
    return dict(stress=stress)


stretch_rate = 2.0
span_rate = 2.0 / 3.0
stream_rate = 0.25


def wall_coefficients(count):
    node_index = jnp.arange(count + 1, dtype=jnp.int32)
    xi_left = (2 * node_index - count - 1).astype(jnp.float32) / (count + 1)
    xi_right = (2 * node_index - count + 1).astype(jnp.float32) / (count + 1)
    spacing = jnp.sinh(2.0 * stretch_rate / (count + 1)) / (
        jnp.tanh(stretch_rate) * jnp.cosh(stretch_rate * xi_left) * jnp.cosh(stretch_rate * xi_right))
    gap_before = spacing[:-1]
    gap_after = spacing[1:]
    lower_band = gap_after / (gap_before + gap_after)
    upper_band = gap_before / (gap_before + gap_after)
    weight = 0.5 * gap_before * gap_after
    return lower_band, upper_band, weight


def wave_squares(length, offset, block_width, mode_ids):
    mode_index = offset + jnp.arange(block_width, dtype=jnp.int32)
    signed = jnp.where(mode_index >= length // 2, mode_index - length, mode_index)
    span_wave = signed.astype(jnp.float32) * span_rate
    stream_wave = mode_ids.astype(jnp.float32) * stream_rate
    wave_sq = stream_wave[:, None] ** 2 + span_wave[None, :] ** 2
    return wave_sq, span_wave ** 2


def thomas(lower_band, upper_band, weight, wave_sq, rows):
    def forward(state, row_data):
        ratio_prev, value_prev = state
        low_entry, upp_entry, wei_entry, row_now = row_data
        pivot_value = 1.0 + wave_sq * wei_entry + low_entry * ratio_prev
        ratio_new = -upp_entry / pivot_value
        value_new = (row_now + low_entry * value_prev) / pivot_value
        return (ratio_new, value_new), (ratio_new, value_new)

    start_state = (jnp.zeros(rows.shape[2:], jnp.float32), jnp.zeros(rows.shape[1:], jnp.float32))
    final_state, sweeps = lax.scan(forward, start_state, (lower_band, upper_band, weight, rows))

    def backward(after_value, row_data):
        ratio_now, value_now = row_data
        value_here = value_now - ratio_now[None] * after_value
        return value_here, value_here

    final_value, solution = lax.scan(backward, jnp.zeros(rows.shape[1:], jnp.float32), sweeps, reverse=True)
    return solution


def reference(stress):
    lower_band, upper_band, weight = wall_coefficients(NY)
    wave_sq, span_sq = wave_squares(NZ, 0, NZ, jnp.arange(KX, dtype=jnp.int32))
    complex_field = lax.complex(stress[0], stress[1])
    transformed = jnp.fft.fft(complex_field, axis=-1)
    spectral = jnp.stack([jnp.real(transformed), jnp.imag(transformed)], axis=0)
    spectral = jnp.transpose(spectral, (2, 0, 1, 3))
    source = spectral * weight[:, None, None, None] * span_sq[None, None, None, :]
    solution = thomas(lower_band, upper_band, weight, wave_sq, source)
    solved_complex = lax.complex(solution[:, 0], solution[:, 1])
    physical = jnp.fft.ifft(solved_complex, axis=-1)
    stacked = jnp.stack([jnp.real(physical), jnp.imag(physical)], axis=0)
    return jnp.transpose(stacked, (0, 2, 1, 3)).astype(jnp.float32)
```

```python
import math

import jax
import jax.numpy as jnp
import ml_dtypes
import numpy as np
from jax import lax
from jax.experimental import pallas as pl
from jax.experimental.pallas import tpu as pltpu
from jax.sharding import PartitionSpec as P

MESH = pl.DeviceIdType.MESH
F32 = jnp.float32
BF16 = jnp.bfloat16

NZ, NY, KX = 2048, 1024, 32
SPAN, WALL = 16, 8
ROWS = NY // WALL
CELLS = NZ // SPAN
MODES = KX // SPAN
LAST = ROWS - 1
STRETCH = 2.0
UNROLL = 8

OFFSETS = [(2, 2), (1, 1), (3, 3), (0, 2), (1, 3), (3, 1), (2, 0), (2, 1), (1, 2), (2, 3), (3, 2),
           (0, 1), (1, 0), (0, 3), (3, 0)]


def tables():
    index = np.arange(CELLS)
    angle = 2.0 * math.pi * (np.outer(index, index) % CELLS) / CELLS
    cos, sin = np.cos(angle), np.sin(angle)
    there = np.block([[cos, -sin], [sin, cos]])
    back = np.block([[cos, sin], [-sin, cos]]) / NZ
    mats = []
    for full in (there, back):
        high = full.astype(np.float32).astype(ml_dtypes.bfloat16)
        mats += [high, (full - high.astype(np.float64)).astype(ml_dtypes.bfloat16)]
    twist = 2.0 * math.pi * np.outer(np.arange(SPAN), index) / NZ
    return np.stack(mats), np.stack([np.cos(twist), np.sin(twist)]).astype(np.float32)


def times(value, cos, sin):
    re, im = value
    return re * cos - im * sin, re * sin + im * cos


def four(x, sign):
    (ar, ai), (br, bi), (cr, ci), (dr, di) = x
    er, ei, fr, fi = ar + cr, ai + ci, ar - cr, ai - ci
    gr, gi, hr, hi = br + dr, bi + di, br - dr, bi - di
    if sign > 0:
        return [(er + gr, ei + gi), (fr - hi, fi + hr), (er - gr, ei - gi), (fr + hi, fi - hr)]
    return [(er + gr, ei + gi), (fr + hi, fi - hr), (er - gr, ei - gi), (fr - hi, fi + hr)]


def sixteen(x, sign):
    half = math.sqrt(0.5)
    first = [four([x[4 * i + j] for i in range(4)], sign) for j in range(4)]
    out = [None] * 16
    for k in range(4):
        col = []
        for j in range(4):
            re, im = first[j][k]
            power = j * k
            if power == 0:
                col.append((re, im))
            elif power == 2:
                col.append(((re - sign * im) * half, (im + sign * re) * half))
            elif power == 4:
                col.append((-im, re) if sign > 0 else (im, -re))
            elif power == 6:
                col.append(((-re - sign * im) * half, (sign * re - im) * half))
            else:
                angle = 2.0 * math.pi * power / 16
                col.append(times((re, im), math.cos(angle), sign * math.sin(angle)))
        for p, value in enumerate(four(col, sign)):
            out[k + 4 * p] = value
    return out


def product(x, high, low):
    x_high = x.astype(BF16)
    x_low = (x - x_high.astype(F32)).astype(BF16)
    dot = lambda a, b: jnp.dot(a, b, preferred_element_type=F32)
    return dot(x_high, high) + (dot(x_low, high) + dot(x_high, low))


def kernel(x_ref, mats_hbm, twist_hbm, o_ref, land, stage, grid, spec, vals, low_s, upp_s, wei_s,
           t_gain, t_carry, t_ratio, t_above, t_below, lhs, sep, rhs, solved, seps, mats, twist,
           there_s, there_r, back_s, back_r, wall_s, wall_r, local):
    me = lax.axis_index("span")
    wall = lax.axis_index("wall")
    y, z = me // 4, me % 4

    def peer(offset):
        return lax.rem(y + offset[0], 4) * 4 + lax.rem(z + offset[1], 4)

    barrier = pltpu.get_barrier_semaphore()
    for offset in OFFSETS:
        pl.semaphore_signal(barrier, inc=1, device_id={"span": peer(offset)}, device_id_type=MESH)
    for k in range(1, WALL):
        pl.semaphore_signal(barrier, inc=1, device_id={"wall": lax.rem(wall + k, WALL)}, device_id_type=MESH)
    pl.semaphore_wait(barrier, SPAN - 1 + WALL - 1)

    there, back = {}, {}
    for mode in range(MODES):
        for j, offset in enumerate(OFFSETS):
            to = peer(offset)
            there[mode, j] = pltpu.make_async_remote_copy(
                src_ref=x_ref.at[:, MODES * to + mode], dst_ref=land.at[mode, me],
                send_sem=there_s.at[mode, j], recv_sem=there_r.at[mode, j],
                device_id={"span": to}, device_id_type=MESH)
            back[mode, j] = pltpu.make_async_remote_copy(
                src_ref=stage.at[mode, to], dst_ref=o_ref.at[:, MODES * me + mode],
                send_sem=back_s.at[mode, j], recv_sem=back_r.at[mode, j],
                device_id={"span": to}, device_id_type=MESH)
    for mode in range(MODES):
        for j in range(len(OFFSETS)):
            there[mode, j].start()
    own = [pltpu.make_async_copy(x_ref.at[:, MODES * me + mode], land.at[mode, me], local.at[mode])
           for mode in range(MODES)]
    consts = [pltpu.make_async_copy(mats_hbm, mats, local.at[2]), pltpu.make_async_copy(twist_hbm, twist, local.at[3])]
    for copy in own + consts:
        copy.start()

    scale = math.sinh(2.0 * STRETCH / (NY + 1)) / math.tanh(STRETCH)

    def bands(cell):
        def cosh(k):
            xi = (2 * (cell + k) - (NY + 1)).astype(F32) * F32(STRETCH / (NY + 1))
            return 0.5 * (jnp.exp(xi) + jnp.exp(-xi))
        c0, c1, c2 = cosh(0), cosh(1), cosh(2)
        total = c0 + c2
        return c0 / total, c2 / total, (0.5 * scale * scale) / (c0 * c2 * (c1 * c1))

    cell = lax.broadcasted_iota(jnp.int32, (ROWS, 128), 0) + wall * ROWS
    low, upp, wei = bands(cell)
    low_s[...] = low
    upp_s[...] = upp
    wei_s[...] = wei
    sep_cell = lax.broadcasted_iota(jnp.int32, (WALL, 128), 0) * ROWS + LAST
    _, sep_upp, _ = bands(sep_cell)
    seps[...] = sep_upp

    freq = lax.broadcasted_iota(jnp.int32, (SPAN, CELLS), 1) * SPAN + lax.broadcasted_iota(jnp.int32, (SPAN, CELLS), 0)
    freq = jnp.where(freq >= NZ // 2, freq - NZ, freq)
    span_sq = jnp.square(freq.astype(F32) * F32(2.0 / 3.0))
    wave = [span_sq + jnp.square((me * MODES + mode).astype(F32) * F32(0.25)) for mode in range(MODES)]
    one = jnp.ones((SPAN, CELLS), F32)
    zero = jnp.zeros((SPAN, CELLS), F32)

    def at(row):
        return pl.ds(pl.multiple_of(row * SPAN, SPAN), SPAN)

    def row_of(ref, row):
        return jnp.broadcast_to(ref[pl.ds(row, 1), :], (SPAN, CELLS))

    def down(row, tops):
        low, upp, wei = row_of(low_s, row), row_of(upp_s, row), row_of(wei_s, row)
        new = []
        for mode in range(MODES):
            d = wave[mode] * wei + low * tops[mode]
            inv = 1.0 / (d + upp)
            t_gain[mode, at(row), :] = span_sq * (wei * inv)
            t_carry[mode, at(row), :] = low * inv
            t_ratio[mode, at(row), :] = upp * inv
            new.append(d * inv)
        return tuple(new)

    tops = lax.fori_loop(0, LAST, down, (one,) * MODES)
    low_l, wei_l = row_of(low_s, LAST), row_of(wei_s, LAST)
    for mode in range(MODES):
        lhs[wall, mode, 0] = wave[mode] * wei_l + low_l * tops[mode]
        t_gain[mode, at(LAST), :] = zero
        t_carry[mode, at(LAST), :] = zero
        t_ratio[mode, at(LAST), :] = zero
        t_above[mode, at(LAST), :] = zero
        t_below[mode, at(LAST), :] = one

    def up(i, state):
        row = LAST - 1 - i
        low, upp, wei = row_of(low_s, row), row_of(upp_s, row), row_of(wei_s, row)
        new = []
        for mode in range(MODES):
            under, below = state[mode]
            e = wave[mode] * wei + upp * under
            inv = 1.0 / (e + low)
            t_above[mode, at(row), :] = low * inv
            below = below * t_ratio[mode, at(row), :]
            t_below[mode, at(row), :] = below
            new.append((e * inv, below))
        return tuple(new)

    ends = lax.fori_loop(0, LAST, up, ((one, one),) * MODES)

    def across(row, state):
        new = []
        for mode in range(MODES):
            above = state[mode] * t_above[mode, at(row), :]
            t_above[mode, at(row), :] = above
            new.append(above)
        return tuple(new)

    above = lax.fori_loop(0, LAST, across, (one,) * MODES)
    for mode in range(MODES):
        lhs[wall, mode, 1] = low_l * above[mode]
        lhs[wall, mode, 2] = ends[mode][0]
        lhs[wall, mode, 3] = ends[mode][1]

    def to_wall(ref, group):
        copies = []
        for k in range(1, WALL):
            copy = pltpu.make_async_remote_copy(
                src_ref=ref, dst_ref=ref, send_sem=wall_s.at[group, k], recv_sem=wall_r.at[group, k],
                device_id={"wall": lax.rem(wall + k, WALL)}, device_id_type=MESH)
            copy.start()
            copies.append(copy)
        return copies

    lhs_copies = to_wall(lhs.at[wall], MODES)
    for copy in lhs_copies:
        copy.wait_recv()
    for mode in range(MODES):
        ratio = zero
        for w in range(WALL):
            sep_up = row_of(seps, w)
            last = w == WALL - 1
            pivot = lhs[w, mode, 0] + (sep_up if last else sep_up * lhs[w + 1, mode, 2])
            link = lhs[w, mode, 1]
            inv = 1.0 / (pivot - link * ratio if w else pivot)
            ratio = zero if last else sep_up * lhs[w + 1, mode, 3] * inv
            sep[mode, w, 0] = inv
            sep[mode, w, 1] = link * inv if w else zero
            sep[mode, w, 2] = ratio

    for copy in own + consts:
        copy.wait()
    own = []
    wall_copies = []
    for mode in range(MODES):
        for j in range(len(OFFSETS)):
            there[mode, j].wait_recv()

        def outer(i, carry):
            rows = pl.ds(pl.multiple_of(i * 8, 8), 8)
            block = [(land[mode, s, 0, rows, :], land[mode, s, 1, rows, :]) for s in range(SPAN)]
            for b, (re, im) in enumerate(sixteen(block, -1)):
                cos = jnp.broadcast_to(twist[0, b:b + 1, :], (8, CELLS))
                sin = jnp.broadcast_to(twist[1, b:b + 1, :], (8, CELLS))
                into = pl.ds(pl.multiple_of(b * ROWS + i * 8, 8), 8)
                grid[0, into, :] = re * cos + im * sin
                grid[1, into, :] = im * cos - re * sin
            return carry

        lax.fori_loop(0, ROWS // 8, outer, 0)

        def inner(i, carry):
            rows = pl.ds(pl.multiple_of(i * 512, 512), 512)
            both = product(jnp.concatenate([grid[0, rows, :], grid[1, rows, :]], axis=1), mats[0], mats[1])
            spec[0, rows, :] = both[:, :CELLS]
            spec[1, rows, :] = both[:, CELLS:]
            return carry

        lax.fori_loop(0, NZ // 512, inner, 0)

        def forward(i, state):
            prev = list(state)
            for k in range(UNROLL):
                row = i * UNROLL + k
                gain, carry = t_gain[mode, at(row), :], t_carry[mode, at(row), :]
                for c in range(2):
                    prev[c] = spec[c, pl.ds(row, SPAN, stride=ROWS), :] * gain + carry * prev[c]
                    vals[c, at(row), :] = prev[c]
            return tuple(prev)

        lax.fori_loop(0, ROWS // UNROLL, forward, (zero, zero))

        def backward(i, state):
            after = list(state)
            for k in range(UNROLL):
                row = LAST - (i * UNROLL + k)
                ratio = t_ratio[mode, at(row), :]
                for c in range(2):
                    after[c] = vals[c, at(row), :] + ratio * after[c]
                    vals[c, at(row), :] = after[c]
            return tuple(after)

        final = [vals[c, at(LAST - 1), :] for c in range(2)]
        first = lax.fori_loop(0, ROWS // UNROLL, backward, (zero, zero))
        for c in range(2):
            source = spec[c, pl.ds(LAST, SPAN, stride=ROWS), :] * (span_sq * wei_l)
            rhs[mode, wall, 0, c] = source + low_l * final[c]
            rhs[mode, wall, 1, c] = first[c]
        copies = to_wall(rhs.at[mode, wall], mode)
        wall_copies += copies
        for copy in copies:
            copy.wait_recv()

        for c in range(2):
            value, values = None, []
            for w in range(WALL):
                r = rhs[mode, w, 0, c]
                if w < WALL - 1:
                    r = r + row_of(seps, w) * rhs[mode, w + 1, 1, c]
                value = r * sep[mode, w, 0] if w == 0 else r * sep[mode, w, 0] + sep[mode, w, 1] * value
                values.append(value)
            for w in range(WALL - 2, -1, -1):
                values[w] = values[w] + sep[mode, w, 2] * values[w + 1]
            for w in range(WALL):
                solved[w, c] = values[w]
        here = [solved[wall, c] for c in range(2)]
        up_at = lax.rem(wall + WALL - 1, WALL)
        there_is = (wall > 0).astype(F32)
        over = [solved[up_at, c] * there_is for c in range(2)]

        def inner_back(i, carry):
            rows = pl.ds(pl.multiple_of(i * 512, 512), 512)
            shape = (512 // SPAN, SPAN, CELLS)
            above = t_above[mode, rows, :].reshape(shape)
            below = t_below[mode, rows, :].reshape(shape)
            parts = [
                (vals[c, rows, :].reshape(shape) + above * over[c][None] + below * here[c][None]).reshape(512, CELLS)
                for c in range(2)]
            both = product(jnp.concatenate(parts, axis=1), mats[2], mats[3])
            re, im = both[:, :CELLS].reshape(shape), both[:, CELLS:].reshape(shape)
            cos, sin = twist[0][None], twist[1][None]
            grid[0, rows, :] = (re * cos - im * sin).reshape(512, CELLS)
            grid[1, rows, :] = (re * sin + im * cos).reshape(512, CELLS)
            return carry

        lax.fori_loop(0, NZ // 512, inner_back, 0)

        def outer_back(i, carry):
            block = [(grid[0, pl.ds(i * (8 * SPAN) + b, 8, stride=SPAN), :],
                      grid[1, pl.ds(i * (8 * SPAN) + b, 8, stride=SPAN), :]) for b in range(SPAN)]
            rows = pl.ds(pl.multiple_of(i * 8, 8), 8)
            for s, (re, im) in enumerate(sixteen(block, 1)):
                stage[mode, s, 0, rows, :] = re
                stage[mode, s, 1, rows, :] = im
            return carry

        lax.fori_loop(0, ROWS // 8, outer_back, 0)

        if mode == 0:
            for m in range(MODES):
                for j in range(len(OFFSETS)):
                    there[m, j].wait_send()
        for j in range(len(OFFSETS)):
            back[mode, j].start()
        copy = pltpu.make_async_copy(stage.at[mode, me], o_ref.at[:, MODES * me + mode], local.at[mode])
        copy.start()
        own.append(copy)

    for copy in lhs_copies + wall_copies:
        copy.wait_send()
    for mode in range(MODES):
        own[mode].wait()
        for j in range(len(OFFSETS)):
            back[mode, j].wait()


def solution(mesh):
    mats, twist = tables()

    def body(stress):
        vmem = lambda *shape: pltpu.VMEM(shape, F32)
        dma = lambda *shape: pltpu.SemaphoreType.DMA(shape)
        table = (MODES, NZ * ROWS // CELLS, CELLS)
        return pl.pallas_call(
            kernel,
            out_shape=jax.ShapeDtypeStruct(stress.shape, F32),
            in_specs=[pl.BlockSpec(memory_space=pltpu.HBM)] * 3,
            out_specs=pl.BlockSpec(memory_space=pltpu.VMEM),
            scratch_shapes=[
                vmem(MODES, SPAN, 2, ROWS, CELLS),
                vmem(MODES, SPAN, 2, ROWS, CELLS),
                vmem(2, SPAN * ROWS, CELLS),
                vmem(2, SPAN * ROWS, CELLS),
                vmem(2, SPAN * ROWS, CELLS),
                vmem(ROWS, 128), vmem(ROWS, 128), vmem(ROWS, 128),
                vmem(*table), vmem(*table), vmem(*table), vmem(*table), vmem(*table),
                vmem(WALL, MODES, 4, SPAN, CELLS),
                vmem(MODES, WALL, 3, SPAN, CELLS),
                vmem(MODES, WALL, 2, 2, SPAN, CELLS),
                vmem(WALL, 2, SPAN, CELLS),
                vmem(WALL, 128),
                pltpu.VMEM((4, 2 * CELLS, 2 * CELLS), BF16),
                vmem(2, SPAN, CELLS),
                dma(MODES, SPAN), dma(MODES, SPAN), dma(MODES, SPAN), dma(MODES, SPAN),
                dma(MODES + 1, WALL), dma(MODES + 1, WALL), dma(4),
            ],
            name="pressure",
            compiler_params=pltpu.CompilerParams(
                collective_id=1, has_side_effects=True, vmem_limit_bytes=56 << 20),
        )(stress, mats, twist)

    placed = P(None, None, "wall", "span")
    return jax.shard_map(body, mesh=mesh, in_specs=(placed,), out_specs=placed, check_vma=False)
```

```python
import math

import jax
import jax.numpy as jnp
from jax import lax
from jax.experimental import pallas as pl
from jax.experimental.pallas import tpu as pltpu
from jax.sharding import PartitionSpec as P

MESH = pl.DeviceIdType.MESH
F32 = jnp.float32
BF16 = jnp.bfloat16

NZ, NY, KX = 2048, 1024, 32
SPAN, WALL = 16, 8
ROWS = NY // WALL
CELLS = NZ // SPAN
MODES = KX // SPAN
LAST = ROWS - 1
STRETCH = 2.0
UNROLL = 8

OFFSETS = [(2, 2), (1, 1), (3, 3), (0, 2), (1, 3), (3, 1), (2, 0), (2, 1), (1, 2), (2, 3), (3, 2),
           (0, 1), (1, 0), (0, 3), (3, 0)]
PIECES = [(offset, part) for part in range(2) for offset in OFFSETS]


def times(value, cos, sin):
    re, im = value
    return re * cos - im * sin, re * sin + im * cos


def four(x, sign):
    (ar, ai), (br, bi), (cr, ci), (dr, di) = x
    er, ei, fr, fi = ar + cr, ai + ci, ar - cr, ai - ci
    gr, gi, hr, hi = br + dr, bi + di, br - dr, bi - di
    if sign > 0:
        return [(er + gr, ei + gi), (fr - hi, fi + hr), (er - gr, ei - gi), (fr + hi, fi - hr)]
    return [(er + gr, ei + gi), (fr + hi, fi - hr), (er - gr, ei - gi), (fr - hi, fi + hr)]


def sixteen(x, sign):
    half = math.sqrt(0.5)
    first = [four([x[4 * i + j] for i in range(4)], sign) for j in range(4)]
    out = [None] * 16
    for k in range(4):
        col = []
        for j in range(4):
            re, im = first[j][k]
            power = j * k
            if power == 0:
                col.append((re, im))
            elif power == 2:
                col.append(((re - sign * im) * half, (im + sign * re) * half))
            elif power == 4:
                col.append((-im, re) if sign > 0 else (im, -re))
            elif power == 6:
                col.append(((-re - sign * im) * half, (sign * re - im) * half))
            else:
                angle = 2.0 * math.pi * power / 16
                col.append(times((re, im), math.cos(angle), sign * math.sin(angle)))
        for p, value in enumerate(four(col, sign)):
            out[k + 4 * p] = value
    return out


def product(x, high, low):
    x_high = x.astype(BF16)
    x_low = (x - x_high.astype(F32)).astype(BF16)
    dot = lambda a, b: jnp.dot(a, b, preferred_element_type=F32)
    return dot(x_high, high) + (dot(x_low, high) + dot(x_high, low))


def kernel(x_ref, o_ref, land, stage, grid, spec, vals, low_s, upp_s, wei_s,
           t_gain, t_carry, t_ratio, t_above, t_below, lhs, sep, rhs, solved, seps, mats, twist,
           there_s, there_r, back_s, back_r, wall_s, wall_r, local):
    me = lax.axis_index("span")
    wall = lax.axis_index("wall")
    y, z = me // 4, me % 4

    def peer(offset):
        return lax.rem(y + offset[0], 4) * 4 + lax.rem(z + offset[1], 4)

    barrier = pltpu.get_barrier_semaphore()
    for offset in OFFSETS:
        pl.semaphore_signal(barrier, inc=1, device_id={"span": peer(offset)}, device_id_type=MESH)
    for k in range(1, WALL):
        pl.semaphore_signal(barrier, inc=1, device_id={"wall": lax.rem(wall + k, WALL)}, device_id_type=MESH)
    pl.semaphore_wait(barrier, SPAN - 1 + WALL - 1)

    there, back = {}, {}
    for mode in range(MODES):
        for j, (offset, part) in enumerate(PIECES):
            to = peer(offset)
            there[mode, j] = pltpu.make_async_remote_copy(
                src_ref=x_ref.at[part, MODES * to + mode], dst_ref=land.at[mode, me, part],
                send_sem=there_s.at[mode, j], recv_sem=there_r.at[mode, j],
                device_id={"span": to}, device_id_type=MESH)
            back[mode, j] = pltpu.make_async_remote_copy(
                src_ref=stage.at[mode, to, part], dst_ref=o_ref.at[part, MODES * me + mode],
                send_sem=back_s.at[mode, j], recv_sem=back_r.at[mode, j],
                device_id={"span": to}, device_id_type=MESH)
    for mode in range(MODES):
        for j in range(len(PIECES)):
            there[mode, j].start()
    own = [pltpu.make_async_copy(x_ref.at[:, MODES * me + mode], land.at[mode, me], local.at[mode])
           for mode in range(MODES)]
    for copy in own:
        copy.start()

    def circle(rows, length):
        shape = (rows, CELLS)
        steps = lax.broadcasted_iota(jnp.int32, shape, 0) * lax.broadcasted_iota(jnp.int32, shape, 1)
        angle = lax.rem(steps, length).astype(F32) * F32(2.0 * math.pi / length)
        return jnp.cos(angle), jnp.sin(angle)

    twist[0], twist[1] = circle(SPAN, NZ)
    cos, sin = circle(CELLS, CELLS)
    for which, (re, im) in enumerate([(cos, -sin), (cos * F32(1 / NZ), sin * F32(1 / NZ))]):
        for r, c, value in [(0, 0, re), (0, 1, im), (1, 0, -im), (1, 1, re)]:
            high = value.astype(BF16)
            place = (pl.ds(r * CELLS, CELLS), pl.ds(c * CELLS, CELLS))
            mats[2 * which, *place] = high
            mats[2 * which + 1, *place] = (value - high.astype(F32)).astype(BF16)

    scale = math.sinh(2.0 * STRETCH / (NY + 1)) / math.tanh(STRETCH)

    def bands(cell):
        def cosh(k):
            xi = (2 * (cell + k) - (NY + 1)).astype(F32) * F32(STRETCH / (NY + 1))
            return 0.5 * (jnp.exp(xi) + jnp.exp(-xi))
        c0, c1, c2 = cosh(0), cosh(1), cosh(2)
        total = c0 + c2
        return c0 / total, c2 / total, (0.5 * scale * scale) / (c0 * c2 * (c1 * c1))

    cell = lax.broadcasted_iota(jnp.int32, (ROWS, 128), 0) + wall * ROWS
    low, upp, wei = bands(cell)
    low_s[...] = low
    upp_s[...] = upp
    wei_s[...] = wei
    sep_cell = lax.broadcasted_iota(jnp.int32, (WALL, 128), 0) * ROWS + LAST
    _, sep_upp, _ = bands(sep_cell)
    seps[...] = sep_upp

    freq = lax.broadcasted_iota(jnp.int32, (SPAN, CELLS), 1) * SPAN + lax.broadcasted_iota(jnp.int32, (SPAN, CELLS), 0)
    freq = jnp.where(freq >= NZ // 2, freq - NZ, freq)
    span_sq = jnp.square(freq.astype(F32) * F32(2.0 / 3.0))
    wave = [span_sq + jnp.square((me * MODES + mode).astype(F32) * F32(0.25)) for mode in range(MODES)]
    one = jnp.ones((SPAN, CELLS), F32)
    zero = jnp.zeros((SPAN, CELLS), F32)

    def at(row):
        return pl.ds(pl.multiple_of(row * SPAN, SPAN), SPAN)

    def row_of(ref, row):
        return jnp.broadcast_to(ref[pl.ds(row, 1), :], (SPAN, CELLS))

    def down(row, tops):
        low, upp, wei = row_of(low_s, row), row_of(upp_s, row), row_of(wei_s, row)
        new = []
        for mode in range(MODES):
            d = wave[mode] * wei + low * tops[mode]
            inv = 1.0 / (d + upp)
            t_gain[mode, at(row), :] = span_sq * (wei * inv)
            t_carry[mode, at(row), :] = low * inv
            t_ratio[mode, at(row), :] = upp * inv
            new.append(d * inv)
        return tuple(new)

    tops = lax.fori_loop(0, LAST, down, (one,) * MODES)
    low_l, wei_l = row_of(low_s, LAST), row_of(wei_s, LAST)
    for mode in range(MODES):
        lhs[wall, mode, 0] = wave[mode] * wei_l + low_l * tops[mode]
        t_gain[mode, at(LAST), :] = zero
        t_carry[mode, at(LAST), :] = zero
        t_ratio[mode, at(LAST), :] = zero
        t_above[mode, at(LAST), :] = zero
        t_below[mode, at(LAST), :] = one

    def up(i, state):
        row = LAST - 1 - i
        low, upp, wei = row_of(low_s, row), row_of(upp_s, row), row_of(wei_s, row)
        new = []
        for mode in range(MODES):
            under, below = state[mode]
            e = wave[mode] * wei + upp * under
            inv = 1.0 / (e + low)
            t_above[mode, at(row), :] = low * inv
            below = below * t_ratio[mode, at(row), :]
            t_below[mode, at(row), :] = below
            new.append((e * inv, below))
        return tuple(new)

    ends = lax.fori_loop(0, LAST, up, ((one, one),) * MODES)

    def across(row, state):
        new = []
        for mode in range(MODES):
            above = state[mode] * t_above[mode, at(row), :]
            t_above[mode, at(row), :] = above
            new.append(above)
        return tuple(new)

    above = lax.fori_loop(0, LAST, across, (one,) * MODES)
    for mode in range(MODES):
        lhs[wall, mode, 1] = low_l * above[mode]
        lhs[wall, mode, 2] = ends[mode][0]
        lhs[wall, mode, 3] = ends[mode][1]

    def to_wall(ref, group):
        copies = []
        for k in range(1, WALL):
            copy = pltpu.make_async_remote_copy(
                src_ref=ref, dst_ref=ref, send_sem=wall_s.at[group, k], recv_sem=wall_r.at[group, k],
                device_id={"wall": lax.rem(wall + k, WALL)}, device_id_type=MESH)
            copy.start()
            copies.append(copy)
        return copies

    lhs_copies = to_wall(lhs.at[wall], MODES)
    for copy in lhs_copies:
        copy.wait_recv()
    for mode in range(MODES):
        ratio = zero
        for w in range(WALL):
            sep_up = row_of(seps, w)
            last = w == WALL - 1
            pivot = lhs[w, mode, 0] + (sep_up if last else sep_up * lhs[w + 1, mode, 2])
            link = lhs[w, mode, 1]
            inv = 1.0 / (pivot - link * ratio if w else pivot)
            ratio = zero if last else sep_up * lhs[w + 1, mode, 3] * inv
            sep[mode, w, 0] = inv
            sep[mode, w, 1] = link * inv if w else zero
            sep[mode, w, 2] = ratio

    for copy in own:
        copy.wait()
    own = []
    wall_copies = []
    for mode in range(MODES):
        for j in range(len(PIECES)):
            there[mode, j].wait_recv()

        def outer(i, carry):
            rows = pl.ds(pl.multiple_of(i * 8, 8), 8)
            block = [(land[mode, s, 0, rows, :], land[mode, s, 1, rows, :]) for s in range(SPAN)]
            for b, (re, im) in enumerate(sixteen(block, -1)):
                cos = jnp.broadcast_to(twist[0, b:b + 1, :], (8, CELLS))
                sin = jnp.broadcast_to(twist[1, b:b + 1, :], (8, CELLS))
                into = pl.ds(pl.multiple_of(b * ROWS + i * 8, 8), 8)
                grid[0, into, :] = re * cos + im * sin
                grid[1, into, :] = im * cos - re * sin
            return carry

        lax.fori_loop(0, ROWS // 8, outer, 0)

        def inner(i, carry):
            rows = pl.ds(pl.multiple_of(i * 512, 512), 512)
            both = product(jnp.concatenate([grid[0, rows, :], grid[1, rows, :]], axis=1), mats[0], mats[1])
            spec[0, rows, :] = both[:, :CELLS]
            spec[1, rows, :] = both[:, CELLS:]
            return carry

        lax.fori_loop(0, NZ // 512, inner, 0)

        def forward(i, state):
            prev = list(state)
            for k in range(UNROLL):
                row = i * UNROLL + k
                gain, carry = t_gain[mode, at(row), :], t_carry[mode, at(row), :]
                for c in range(2):
                    prev[c] = spec[c, pl.ds(row, SPAN, stride=ROWS), :] * gain + carry * prev[c]
                    vals[c, at(row), :] = prev[c]
            return tuple(prev)

        lax.fori_loop(0, ROWS // UNROLL, forward, (zero, zero))

        def backward(i, state):
            after = list(state)
            for k in range(UNROLL):
                row = LAST - (i * UNROLL + k)
                ratio = t_ratio[mode, at(row), :]
                for c in range(2):
                    after[c] = vals[c, at(row), :] + ratio * after[c]
                    vals[c, at(row), :] = after[c]
            return tuple(after)

        final = [vals[c, at(LAST - 1), :] for c in range(2)]
        first = lax.fori_loop(0, ROWS // UNROLL, backward, (zero, zero))
        for c in range(2):
            source = spec[c, pl.ds(LAST, SPAN, stride=ROWS), :] * (span_sq * wei_l)
            rhs[mode, wall, 0, c] = source + low_l * final[c]
            rhs[mode, wall, 1, c] = first[c]
        copies = to_wall(rhs.at[mode, wall], mode)
        wall_copies += copies
        for copy in copies:
            copy.wait_recv()

        for c in range(2):
            value, values = None, []
            for w in range(WALL):
                r = rhs[mode, w, 0, c]
                if w < WALL - 1:
                    r = r + row_of(seps, w) * rhs[mode, w + 1, 1, c]
                value = r * sep[mode, w, 0] if w == 0 else r * sep[mode, w, 0] + sep[mode, w, 1] * value
                values.append(value)
            for w in range(WALL - 2, -1, -1):
                values[w] = values[w] + sep[mode, w, 2] * values[w + 1]
            for w in range(WALL):
                solved[w, c] = values[w]
        here = [solved[wall, c] for c in range(2)]
        up_at = lax.rem(wall + WALL - 1, WALL)
        there_is = (wall > 0).astype(F32)
        over = [solved[up_at, c] * there_is for c in range(2)]

        def inner_back(i, carry):
            rows = pl.ds(pl.multiple_of(i * 512, 512), 512)
            shape = (512 // SPAN, SPAN, CELLS)
            above = t_above[mode, rows, :].reshape(shape)
            below = t_below[mode, rows, :].reshape(shape)
            parts = [
                (vals[c, rows, :].reshape(shape) + above * over[c][None] + below * here[c][None]).reshape(512, CELLS)
                for c in range(2)]
            both = product(jnp.concatenate(parts, axis=1), mats[2], mats[3])
            re, im = both[:, :CELLS].reshape(shape), both[:, CELLS:].reshape(shape)
            cos, sin = twist[0][None], twist[1][None]
            grid[0, rows, :] = (re * cos - im * sin).reshape(512, CELLS)
            grid[1, rows, :] = (re * sin + im * cos).reshape(512, CELLS)
            return carry

        lax.fori_loop(0, NZ // 512, inner_back, 0)

        def outer_back(i, carry):
            block = [(grid[0, pl.ds(i * (8 * SPAN) + b, 8, stride=SPAN), :],
                      grid[1, pl.ds(i * (8 * SPAN) + b, 8, stride=SPAN), :]) for b in range(SPAN)]
            rows = pl.ds(pl.multiple_of(i * 8, 8), 8)
            for s, (re, im) in enumerate(sixteen(block, 1)):
                stage[mode, s, 0, rows, :] = re
                stage[mode, s, 1, rows, :] = im
            return carry

        lax.fori_loop(0, ROWS // 8, outer_back, 0)

        if mode == 0:
            for m in range(MODES):
                for j in range(len(PIECES)):
                    there[m, j].wait_send()
        for j in range(len(PIECES)):
            back[mode, j].start()
        copy = pltpu.make_async_copy(stage.at[mode, me], o_ref.at[:, MODES * me + mode], local.at[mode])
        copy.start()
        own.append(copy)

    for copy in lhs_copies + wall_copies:
        copy.wait_send()
    for mode in range(MODES):
        own[mode].wait()
        for j in range(len(PIECES)):
            back[mode, j].wait()


def solution(mesh):
    def body(stress):
        vmem = lambda *shape: pltpu.VMEM(shape, F32)
        dma = lambda *shape: pltpu.SemaphoreType.DMA(shape)
        table = (MODES, NZ * ROWS // CELLS, CELLS)
        return pl.pallas_call(
            kernel,
            out_shape=jax.ShapeDtypeStruct(stress.shape, F32),
            in_specs=[pl.BlockSpec(memory_space=pltpu.HBM)],
            out_specs=pl.BlockSpec(memory_space=pl.ANY),
            scratch_shapes=[
                vmem(MODES, SPAN, 2, ROWS, CELLS),
                vmem(MODES, SPAN, 2, ROWS, CELLS),
                vmem(2, SPAN * ROWS, CELLS),
                vmem(2, SPAN * ROWS, CELLS),
                vmem(2, SPAN * ROWS, CELLS),
                vmem(ROWS, 128), vmem(ROWS, 128), vmem(ROWS, 128),
                vmem(*table), vmem(*table), vmem(*table), vmem(*table), vmem(*table),
                vmem(WALL, MODES, 4, SPAN, CELLS),
                vmem(MODES, WALL, 3, SPAN, CELLS),
                vmem(MODES, WALL, 2, 2, SPAN, CELLS),
                vmem(WALL, 2, SPAN, CELLS),
                vmem(WALL, 128),
                pltpu.VMEM((4, 2 * CELLS, 2 * CELLS), BF16),
                vmem(2, SPAN, CELLS),
                dma(MODES, len(PIECES)), dma(MODES, len(PIECES)), dma(MODES, len(PIECES)), dma(MODES, len(PIECES)),
                dma(MODES + 1, WALL), dma(MODES + 1, WALL), dma(MODES),
            ],
            name="pressure",
            compiler_params=pltpu.CompilerParams(
                collective_id=1, has_side_effects=True, vmem_limit_bytes=48 << 20),
        )(stress)

    placed = P(None, None, "wall", "span")
    return jax.shard_map(body, mesh=mesh, in_specs=(placed,), out_specs=placed, check_vma=False)
```

```python
import math

import jax
import jax.numpy as jnp
from jax import lax
from jax.experimental import pallas as pl
from jax.experimental.pallas import tpu as pltpu
from jax.sharding import PartitionSpec as P

MESH = pl.DeviceIdType.MESH
F32 = jnp.float32
BF16 = jnp.bfloat16

NZ, NY, KX = 2048, 1024, 32
SPAN, WALL = 16, 8
ROWS = NY // WALL
CELLS = NZ // SPAN
MODES = KX // SPAN
LAST = ROWS - 1
STRETCH = 2.0
UNROLL = 8

OFFSETS = [(2, 2), (1, 1), (3, 3), (0, 2), (1, 3), (3, 1), (2, 0), (2, 1), (1, 2), (2, 3), (3, 2),
           (0, 1), (1, 0), (0, 3), (3, 0)]
PIECES = [(offset, part) for part in range(2) for offset in OFFSETS]
EARLY = [(0, j) for j in range(30)] + [(1, j) for j in range(15)]
GATES = (EARLY, [(1, j) for j in range(15, 30)])


def times(value, cos, sin):
    re, im = value
    return re * cos - im * sin, re * sin + im * cos


def four(x, sign):
    (ar, ai), (br, bi), (cr, ci), (dr, di) = x
    er, ei, fr, fi = ar + cr, ai + ci, ar - cr, ai - ci
    gr, gi, hr, hi = br + dr, bi + di, br - dr, bi - di
    if sign > 0:
        return [(er + gr, ei + gi), (fr - hi, fi + hr), (er - gr, ei - gi), (fr + hi, fi - hr)]
    return [(er + gr, ei + gi), (fr + hi, fi - hr), (er - gr, ei - gi), (fr - hi, fi + hr)]


def sixteen(x, sign):
    half = math.sqrt(0.5)
    first = [four([x[4 * i + j] for i in range(4)], sign) for j in range(4)]
    out = [None] * 16
    for k in range(4):
        col = []
        for j in range(4):
            re, im = first[j][k]
            power = j * k
            if power == 0:
                col.append((re, im))
            elif power == 2:
                col.append(((re - sign * im) * half, (im + sign * re) * half))
            elif power == 4:
                col.append((-im, re) if sign > 0 else (im, -re))
            elif power == 6:
                col.append(((-re - sign * im) * half, (sign * re - im) * half))
            else:
                angle = 2.0 * math.pi * power / 16
                col.append(times((re, im), math.cos(angle), sign * math.sin(angle)))
        for p, value in enumerate(four(col, sign)):
            out[k + 4 * p] = value
    return out


def product(x, high, low):
    x_high = x.astype(BF16)
    x_low = (x - x_high.astype(F32)).astype(BF16)
    dot = lambda a, b: jnp.dot(a, b, preferred_element_type=F32)
    return dot(x_high, high) + (dot(x_low, high) + dot(x_high, low))


def kernel(x_ref, o_ref, land, stage, grid, spec, vals, low_s, upp_s, wei_s,
           t_gain, t_carry, t_ratio, t_above, t_below, lhs, sep, rhs, solved, seps, mats, twist,
           there_s, there_r, back_s, back_r, wall_s, wall_r, local):
    me = lax.axis_index("span")
    wall = lax.axis_index("wall")
    y, z = me // 4, me % 4

    def peer(offset):
        return lax.rem(y + offset[0], 4) * 4 + lax.rem(z + offset[1], 4)

    barrier = pltpu.get_barrier_semaphore()
    for offset in OFFSETS:
        pl.semaphore_signal(barrier, inc=1, device_id={"span": peer(offset)}, device_id_type=MESH)
    for k in range(1, WALL):
        pl.semaphore_signal(barrier, inc=1, device_id={"wall": lax.rem(wall + k, WALL)}, device_id_type=MESH)
    pl.semaphore_wait(barrier, SPAN - 1 + WALL - 1)

    there, back = {}, {}
    for mode in range(MODES):
        for j, (offset, part) in enumerate(PIECES):
            to = peer(offset)
            there[mode, j] = pltpu.make_async_remote_copy(
                src_ref=x_ref.at[part, MODES * to + mode], dst_ref=land.at[mode, me, part],
                send_sem=there_s.at[mode, j], recv_sem=there_r.at[mode, j],
                device_id={"span": to}, device_id_type=MESH)
            back[mode, j] = pltpu.make_async_remote_copy(
                src_ref=stage.at[mode, to, part], dst_ref=o_ref.at[part, MODES * me + mode],
                send_sem=back_s.at[mode, j], recv_sem=back_r.at[mode, j],
                device_id={"span": to}, device_id_type=MESH)
    for j in range(len(PIECES)):
        there[0, j].start()
    own = [pltpu.make_async_copy(x_ref.at[:, MODES * me + mode], land.at[mode, me], local.at[mode])
           for mode in range(MODES)]
    for copy in own:
        copy.start()

    def circle(rows, length):
        shape = (rows, CELLS)
        steps = lax.broadcasted_iota(jnp.int32, shape, 0) * lax.broadcasted_iota(jnp.int32, shape, 1)
        angle = lax.rem(steps, length).astype(F32) * F32(2.0 * math.pi / length)
        return jnp.cos(angle), jnp.sin(angle)

    twist[0], twist[1] = circle(SPAN, NZ)
    cos, sin = circle(CELLS, CELLS)
    for which, (re, im) in enumerate([(cos, -sin), (cos * F32(1 / NZ), sin * F32(1 / NZ))]):
        for r, c, value in [(0, 0, re), (0, 1, im), (1, 0, -im), (1, 1, re)]:
            high = value.astype(BF16)
            place = (pl.ds(r * CELLS, CELLS), pl.ds(c * CELLS, CELLS))
            mats[2 * which, *place] = high
            mats[2 * which + 1, *place] = (value - high.astype(F32)).astype(BF16)

    scale = math.sinh(2.0 * STRETCH / (NY + 1)) / math.tanh(STRETCH)

    def bands(cell):
        def cosh(k):
            xi = (2 * (cell + k) - (NY + 1)).astype(F32) * F32(STRETCH / (NY + 1))
            return 0.5 * (jnp.exp(xi) + jnp.exp(-xi))
        c0, c1, c2 = cosh(0), cosh(1), cosh(2)
        total = c0 + c2
        return c0 / total, c2 / total, (0.5 * scale * scale) / (c0 * c2 * (c1 * c1))

    cell = lax.broadcasted_iota(jnp.int32, (ROWS, 128), 0) + wall * ROWS
    low, upp, wei = bands(cell)
    low_s[...] = low
    upp_s[...] = upp
    wei_s[...] = wei
    sep_cell = lax.broadcasted_iota(jnp.int32, (WALL, 128), 0) * ROWS + LAST
    _, sep_upp, _ = bands(sep_cell)
    seps[...] = sep_upp

    freq = lax.broadcasted_iota(jnp.int32, (SPAN, CELLS), 1) * SPAN + lax.broadcasted_iota(jnp.int32, (SPAN, CELLS), 0)
    freq = jnp.where(freq >= NZ // 2, freq - NZ, freq)
    span_sq = jnp.square(freq.astype(F32) * F32(2.0 / 3.0))
    wave = [span_sq + jnp.square((me * MODES + mode).astype(F32) * F32(0.25)) for mode in range(MODES)]
    one = jnp.ones((SPAN, CELLS), F32)
    zero = jnp.zeros((SPAN, CELLS), F32)

    def at(row):
        return pl.ds(pl.multiple_of(row * SPAN, SPAN), SPAN)

    def row_of(ref, row):
        return jnp.broadcast_to(ref[pl.ds(row, 1), :], (SPAN, CELLS))

    def down(row, tops):
        low, upp, wei = row_of(low_s, row), row_of(upp_s, row), row_of(wei_s, row)
        new = []
        for mode in range(MODES):
            d = wave[mode] * wei + low * tops[mode]
            inv = 1.0 / (d + upp)
            t_gain[mode, at(row), :] = span_sq * (wei * inv)
            t_carry[mode, at(row), :] = low * inv
            t_ratio[mode, at(row), :] = upp * inv
            new.append(d * inv)
        return tuple(new)

    tops = lax.fori_loop(0, LAST, down, (one,) * MODES)
    low_l, wei_l = row_of(low_s, LAST), row_of(wei_s, LAST)
    for mode in range(MODES):
        lhs[wall, mode, 0] = wave[mode] * wei_l + low_l * tops[mode]
        t_gain[mode, at(LAST), :] = zero
        t_carry[mode, at(LAST), :] = zero
        t_ratio[mode, at(LAST), :] = zero
        t_above[mode, at(LAST), :] = zero
        t_below[mode, at(LAST), :] = one

    def up(i, state):
        row = LAST - 1 - i
        low, upp, wei = row_of(low_s, row), row_of(upp_s, row), row_of(wei_s, row)
        new = []
        for mode in range(MODES):
            under, below = state[mode]
            e = wave[mode] * wei + upp * under
            inv = 1.0 / (e + low)
            t_above[mode, at(row), :] = low * inv
            below = below * t_ratio[mode, at(row), :]
            t_below[mode, at(row), :] = below
            new.append((e * inv, below))
        return tuple(new)

    ends = lax.fori_loop(0, LAST, up, ((one, one),) * MODES)

    def across(row, state):
        new = []
        for mode in range(MODES):
            above = state[mode] * t_above[mode, at(row), :]
            t_above[mode, at(row), :] = above
            new.append(above)
        return tuple(new)

    above = lax.fori_loop(0, LAST, across, (one,) * MODES)
    for mode in range(MODES):
        lhs[wall, mode, 1] = low_l * above[mode]
        lhs[wall, mode, 2] = ends[mode][0]
        lhs[wall, mode, 3] = ends[mode][1]

    def to_wall(ref, group):
        copies = []
        for k in range(1, WALL):
            copy = pltpu.make_async_remote_copy(
                src_ref=ref, dst_ref=ref, send_sem=wall_s.at[group, k], recv_sem=wall_r.at[group, k],
                device_id={"wall": lax.rem(wall + k, WALL)}, device_id_type=MESH)
            copy.start()
            copies.append(copy)
        return copies

    lhs_copies = to_wall(lhs.at[wall], MODES)
    for j in range(len(PIECES)):
        there[1, j].start()

    def factor():
        for copy in lhs_copies:
            copy.wait_recv()
        for mode in range(MODES):
            ratio = zero
            for w in range(WALL):
                sep_up = row_of(seps, w)
                last = w == WALL - 1
                pivot = lhs[w, mode, 0] + (sep_up if last else sep_up * lhs[w + 1, mode, 2])
                link = lhs[w, mode, 1]
                inv = 1.0 / (pivot - link * ratio if w else pivot)
                ratio = zero if last else sep_up * lhs[w + 1, mode, 3] * inv
                sep[mode, w, 0] = inv
                sep[mode, w, 1] = link * inv if w else zero
                sep[mode, w, 2] = ratio

    for copy in own:
        copy.wait()
    own = []
    wall_copies = []
    for mode in range(MODES):
        for j in range(len(PIECES)):
            there[mode, j].wait_recv()

        def outer(i, carry):
            rows = pl.ds(pl.multiple_of(i * 8, 8), 8)
            block = [(land[mode, s, 0, rows, :], land[mode, s, 1, rows, :]) for s in range(SPAN)]
            for b, (re, im) in enumerate(sixteen(block, -1)):
                cos = jnp.broadcast_to(twist[0, b:b + 1, :], (8, CELLS))
                sin = jnp.broadcast_to(twist[1, b:b + 1, :], (8, CELLS))
                into = pl.ds(pl.multiple_of(b * ROWS + i * 8, 8), 8)
                grid[0, into, :] = re * cos + im * sin
                grid[1, into, :] = im * cos - re * sin
            return carry

        lax.fori_loop(0, ROWS // 8, outer, 0)

        def inner(i, carry):
            rows = pl.ds(pl.multiple_of(i * 512, 512), 512)
            both = product(jnp.concatenate([grid[0, rows, :], grid[1, rows, :]], axis=1), mats[0], mats[1])
            spec[0, rows, :] = both[:, :CELLS]
            spec[1, rows, :] = both[:, CELLS:]
            return carry

        lax.fori_loop(0, NZ // 512, inner, 0)

        def forward(i, state):
            prev = list(state)
            for k in range(UNROLL):
                row = i * UNROLL + k
                gain, carry = t_gain[mode, at(row), :], t_carry[mode, at(row), :]
                for c in range(2):
                    prev[c] = spec[c, pl.ds(row, SPAN, stride=ROWS), :] * gain + carry * prev[c]
                    vals[c, at(row), :] = prev[c]
            return tuple(prev)

        lax.fori_loop(0, ROWS // UNROLL, forward, (zero, zero))

        def backward(i, state):
            after = list(state)
            for k in range(UNROLL):
                row = LAST - (i * UNROLL + k)
                ratio = t_ratio[mode, at(row), :]
                for c in range(2):
                    after[c] = vals[c, at(row), :] + ratio * after[c]
                    vals[c, at(row), :] = after[c]
            return tuple(after)

        final = [vals[c, at(LAST - 1), :] for c in range(2)]
        first = lax.fori_loop(0, ROWS // UNROLL, backward, (zero, zero))
        for c in range(2):
            source = spec[c, pl.ds(LAST, SPAN, stride=ROWS), :] * (span_sq * wei_l)
            rhs[mode, wall, 0, c] = source + low_l * final[c]
            rhs[mode, wall, 1, c] = first[c]
        copies = to_wall(rhs.at[mode, wall], mode)
        wall_copies += copies
        if mode == 0:
            factor()
        for copy in copies:
            copy.wait_recv()

        for c in range(2):
            value, values = None, []
            for w in range(WALL):
                r = rhs[mode, w, 0, c]
                if w < WALL - 1:
                    r = r + row_of(seps, w) * rhs[mode, w + 1, 1, c]
                value = r * sep[mode, w, 0] if w == 0 else r * sep[mode, w, 0] + sep[mode, w, 1] * value
                values.append(value)
            for w in range(WALL - 2, -1, -1):
                values[w] = values[w] + sep[mode, w, 2] * values[w + 1]
            for w in range(WALL):
                solved[w, c] = values[w]
        here = [solved[wall, c] for c in range(2)]
        up_at = lax.rem(wall + WALL - 1, WALL)
        there_is = (wall > 0).astype(F32)
        over = [solved[up_at, c] * there_is for c in range(2)]

        def inner_back(i, carry):
            rows = pl.ds(pl.multiple_of(i * 512, 512), 512)
            shape = (512 // SPAN, SPAN, CELLS)
            above = t_above[mode, rows, :].reshape(shape)
            below = t_below[mode, rows, :].reshape(shape)
            parts = [
                (vals[c, rows, :].reshape(shape) + above * over[c][None] + below * here[c][None]).reshape(512, CELLS)
                for c in range(2)]
            both = product(jnp.concatenate(parts, axis=1), mats[2], mats[3])
            re, im = both[:, :CELLS].reshape(shape), both[:, CELLS:].reshape(shape)
            cos, sin = twist[0][None], twist[1][None]
            grid[0, rows, :] = (re * cos - im * sin).reshape(512, CELLS)
            grid[1, rows, :] = (re * sin + im * cos).reshape(512, CELLS)
            return carry

        lax.fori_loop(0, NZ // 512, inner_back, 0)

        def outer_back(i, carry):
            block = [(grid[0, pl.ds(i * (8 * SPAN) + b, 8, stride=SPAN), :],
                      grid[1, pl.ds(i * (8 * SPAN) + b, 8, stride=SPAN), :]) for b in range(SPAN)]
            rows = pl.ds(pl.multiple_of(i * 8, 8), 8)
            for s, (re, im) in enumerate(sixteen(block, 1)):
                stage[mode, s, 0, rows, :] = re
                stage[mode, s, 1, rows, :] = im
            return carry

        lax.fori_loop(0, ROWS // 8, outer_back, 0)

        for m, j in GATES[mode]:
            there[m, j].wait_send()
        for j in range(len(PIECES)):
            back[mode, j].start()
        copy = pltpu.make_async_copy(stage.at[mode, me], o_ref.at[:, MODES * me + mode], local.at[mode])
        copy.start()
        own.append(copy)

    for copy in lhs_copies + wall_copies:
        copy.wait_send()
    for mode in range(MODES):
        own[mode].wait()
        for j in range(len(PIECES)):
            back[mode, j].wait()


def solution(mesh):
    def body(stress):
        vmem = lambda *shape: pltpu.VMEM(shape, F32)
        dma = lambda *shape: pltpu.SemaphoreType.DMA(shape)
        table = (MODES, NZ * ROWS // CELLS, CELLS)
        return pl.pallas_call(
            kernel,
            out_shape=jax.ShapeDtypeStruct(stress.shape, F32),
            in_specs=[pl.BlockSpec(memory_space=pltpu.HBM)],
            out_specs=pl.BlockSpec(memory_space=pl.ANY),
            scratch_shapes=[
                vmem(MODES, SPAN, 2, ROWS, CELLS),
                vmem(MODES, SPAN, 2, ROWS, CELLS),
                vmem(2, SPAN * ROWS, CELLS),
                vmem(2, SPAN * ROWS, CELLS),
                vmem(2, SPAN * ROWS, CELLS),
                vmem(ROWS, 128), vmem(ROWS, 128), vmem(ROWS, 128),
                vmem(*table), vmem(*table), vmem(*table), vmem(*table), vmem(*table),
                vmem(WALL, MODES, 4, SPAN, CELLS),
                vmem(MODES, WALL, 3, SPAN, CELLS),
                vmem(MODES, WALL, 2, 2, SPAN, CELLS),
                vmem(WALL, 2, SPAN, CELLS),
                vmem(WALL, 128),
                pltpu.VMEM((4, 2 * CELLS, 2 * CELLS), BF16),
                vmem(2, SPAN, CELLS),
                dma(MODES, len(PIECES)), dma(MODES, len(PIECES)), dma(MODES, len(PIECES)), dma(MODES, len(PIECES)),
                dma(MODES + 1, WALL), dma(MODES + 1, WALL), dma(MODES),
            ],
            name="pressure",
            compiler_params=pltpu.CompilerParams(
                collective_id=1, has_side_effects=True, vmem_limit_bytes=48 << 20),
        )(stress)

    placed = P(None, None, "wall", "span")
    return jax.shard_map(body, mesh=mesh, in_specs=(placed,), out_specs=placed, check_vma=False)
```

```python
import math

import jax
import jax.numpy as jnp
from jax import lax
from jax.experimental import pallas as pl
from jax.experimental.pallas import tpu as pltpu
from jax.sharding import PartitionSpec as P

MESH = pl.DeviceIdType.MESH
F32 = jnp.float32
BF16 = jnp.bfloat16

NZ, NY, KX = 2048, 1024, 32
SPAN, WALL = 16, 8
ROWS = NY // WALL
CELLS = NZ // SPAN
MODES = KX // SPAN
LAST = ROWS - 1
STRETCH = 2.0
UNROLL = 8

OFFSETS = [(2, 2), (1, 1), (3, 3), (0, 2), (1, 3), (3, 1), (2, 0), (2, 1), (1, 2), (2, 3), (3, 2),
           (1, 0), (0, 1), (3, 0), (0, 3)]
PIECES = [(offset, part) for part in range(2) for offset in OFFSETS]
EARLY = [(0, j) for j in range(30)] + [(1, j) for j in range(15)]
HELD = 15
GATES = (EARLY, [(1, j) for j in range(15, 30)])


def times(value, cos, sin):
    re, im = value
    return re * cos - im * sin, re * sin + im * cos


def four(x, sign):
    (ar, ai), (br, bi), (cr, ci), (dr, di) = x
    er, ei, fr, fi = ar + cr, ai + ci, ar - cr, ai - ci
    gr, gi, hr, hi = br + dr, bi + di, br - dr, bi - di
    if sign > 0:
        return [(er + gr, ei + gi), (fr - hi, fi + hr), (er - gr, ei - gi), (fr + hi, fi - hr)]
    return [(er + gr, ei + gi), (fr + hi, fi - hr), (er - gr, ei - gi), (fr - hi, fi + hr)]


def sixteen(x, sign):
    half = math.sqrt(0.5)
    first = [four([x[4 * i + j] for i in range(4)], sign) for j in range(4)]
    out = [None] * 16
    for k in range(4):
        col = []
        for j in range(4):
            re, im = first[j][k]
            power = j * k
            if power == 0:
                col.append((re, im))
            elif power == 2:
                col.append(((re - sign * im) * half, (im + sign * re) * half))
            elif power == 4:
                col.append((-im, re) if sign > 0 else (im, -re))
            elif power == 6:
                col.append(((-re - sign * im) * half, (sign * re - im) * half))
            else:
                angle = 2.0 * math.pi * power / 16
                col.append(times((re, im), math.cos(angle), sign * math.sin(angle)))
        for p, value in enumerate(four(col, sign)):
            out[k + 4 * p] = value
    return out


def product(x, high, low):
    x_high = x.astype(BF16)
    x_low = (x - x_high.astype(F32)).astype(BF16)
    dot = lambda a, b: jnp.dot(a, b, preferred_element_type=F32)
    return dot(x_high, high) + (dot(x_low, high) + dot(x_high, low))


def kernel(x_ref, o_ref, land, stage, grid, spec, vals, low_s, upp_s, wei_s,
           t_gain, t_carry, t_ratio, t_above, t_below, lhs, sep, rhs, solved, seps, mats, twist,
           there_s, there_r, back_s, back_r, wall_s, wall_r, local):
    me = lax.axis_index("span")
    wall = lax.axis_index("wall")
    y, z = me // 4, me % 4

    def peer(offset):
        return lax.rem(y + offset[0], 4) * 4 + lax.rem(z + offset[1], 4)

    barrier = pltpu.get_barrier_semaphore()
    for offset in OFFSETS:
        pl.semaphore_signal(barrier, inc=1, device_id={"span": peer(offset)}, device_id_type=MESH)
    for k in range(1, WALL):
        pl.semaphore_signal(barrier, inc=1, device_id={"wall": lax.rem(wall + k, WALL)}, device_id_type=MESH)
    pl.semaphore_wait(barrier, SPAN - 1 + WALL - 1)

    there, back = {}, {}
    for mode in range(MODES):
        for j, (offset, part) in enumerate(PIECES):
            to = peer(offset)
            there[mode, j] = pltpu.make_async_remote_copy(
                src_ref=x_ref.at[part, MODES * to + mode], dst_ref=land.at[mode, me, part],
                send_sem=there_s.at[mode, j], recv_sem=there_r.at[mode, j],
                device_id={"span": to}, device_id_type=MESH)
            back[mode, j] = pltpu.make_async_remote_copy(
                src_ref=stage.at[mode, to, part], dst_ref=o_ref.at[part, MODES * me + mode],
                send_sem=back_s.at[mode, j], recv_sem=back_r.at[mode, j],
                device_id={"span": to}, device_id_type=MESH)
    for j in range(len(PIECES)):
        there[0, j].start()
    own = [pltpu.make_async_copy(x_ref.at[:, MODES * me + mode], land.at[mode, me], local.at[mode])
           for mode in range(MODES)]
    for copy in own:
        copy.start()

    def circle(rows, length):
        shape = (rows, CELLS)
        steps = lax.broadcasted_iota(jnp.int32, shape, 0) * lax.broadcasted_iota(jnp.int32, shape, 1)
        angle = lax.rem(steps, length).astype(F32) * F32(2.0 * math.pi / length)
        return jnp.cos(angle), jnp.sin(angle)

    twist[0], twist[1] = circle(SPAN, NZ)
    cos, sin = circle(CELLS, CELLS)
    for which, (re, im) in enumerate([(cos, -sin), (cos * F32(1 / NZ), sin * F32(1 / NZ))]):
        for r, c, value in [(0, 0, re), (0, 1, im), (1, 0, -im), (1, 1, re)]:
            high = value.astype(BF16)
            place = (pl.ds(r * CELLS, CELLS), pl.ds(c * CELLS, CELLS))
            mats[2 * which, *place] = high
            mats[2 * which + 1, *place] = (value - high.astype(F32)).astype(BF16)

    scale = math.sinh(2.0 * STRETCH / (NY + 1)) / math.tanh(STRETCH)

    def bands(cell):
        def cosh(k):
            xi = (2 * (cell + k) - (NY + 1)).astype(F32) * F32(STRETCH / (NY + 1))
            return 0.5 * (jnp.exp(xi) + jnp.exp(-xi))
        c0, c1, c2 = cosh(0), cosh(1), cosh(2)
        total = c0 + c2
        return c0 / total, c2 / total, (0.5 * scale * scale) / (c0 * c2 * (c1 * c1))

    cell = lax.broadcasted_iota(jnp.int32, (ROWS, 128), 0) + wall * ROWS
    low, upp, wei = bands(cell)
    low_s[...] = low
    upp_s[...] = upp
    wei_s[...] = wei
    sep_cell = lax.broadcasted_iota(jnp.int32, (WALL, 128), 0) * ROWS + LAST
    _, sep_upp, _ = bands(sep_cell)
    seps[...] = sep_upp

    freq = lax.broadcasted_iota(jnp.int32, (SPAN, CELLS), 1) * SPAN + lax.broadcasted_iota(jnp.int32, (SPAN, CELLS), 0)
    freq = jnp.where(freq >= NZ // 2, freq - NZ, freq)
    span_sq = jnp.square(freq.astype(F32) * F32(2.0 / 3.0))
    wave = [span_sq + jnp.square((me * MODES + mode).astype(F32) * F32(0.25)) for mode in range(MODES)]
    one = jnp.ones((SPAN, CELLS), F32)
    zero = jnp.zeros((SPAN, CELLS), F32)

    def at(row):
        return pl.ds(pl.multiple_of(row * SPAN, SPAN), SPAN)

    def row_of(ref, row):
        return jnp.broadcast_to(ref[pl.ds(row, 1), :], (SPAN, CELLS))

    def down(row, tops):
        low, upp, wei = row_of(low_s, row), row_of(upp_s, row), row_of(wei_s, row)
        new = []
        for mode in range(MODES):
            d = wave[mode] * wei + low * tops[mode]
            inv = 1.0 / (d + upp)
            t_gain[mode, at(row), :] = span_sq * (wei * inv)
            t_carry[mode, at(row), :] = low * inv
            t_ratio[mode, at(row), :] = upp * inv
            new.append(d * inv)
        return tuple(new)

    tops = lax.fori_loop(0, LAST, down, (one,) * MODES)
    low_l, wei_l = row_of(low_s, LAST), row_of(wei_s, LAST)
    for mode in range(MODES):
        lhs[wall, mode, 0] = wave[mode] * wei_l + low_l * tops[mode]
        t_gain[mode, at(LAST), :] = zero
        t_carry[mode, at(LAST), :] = zero
        t_ratio[mode, at(LAST), :] = zero
        t_above[mode, at(LAST), :] = zero
        t_below[mode, at(LAST), :] = one

    def up(i, state):
        row = LAST - 1 - i
        low, upp, wei = row_of(low_s, row), row_of(upp_s, row), row_of(wei_s, row)
        new = []
        for mode in range(MODES):
            under, below = state[mode]
            e = wave[mode] * wei + upp * under
            inv = 1.0 / (e + low)
            t_above[mode, at(row), :] = low * inv
            below = below * t_ratio[mode, at(row), :]
            t_below[mode, at(row), :] = below
            new.append((e * inv, below))
        return tuple(new)

    ends = lax.fori_loop(0, LAST, up, ((one, one),) * MODES)

    def across(row, state):
        new = []
        for mode in range(MODES):
            above = state[mode] * t_above[mode, at(row), :]
            t_above[mode, at(row), :] = above
            new.append(above)
        return tuple(new)

    above = lax.fori_loop(0, LAST, across, (one,) * MODES)
    for mode in range(MODES):
        lhs[wall, mode, 1] = low_l * above[mode]
        lhs[wall, mode, 2] = ends[mode][0]
        lhs[wall, mode, 3] = ends[mode][1]

    def to_wall(ref, group):
        copies = []
        for k in range(1, WALL):
            copy = pltpu.make_async_remote_copy(
                src_ref=ref, dst_ref=ref, send_sem=wall_s.at[group, k], recv_sem=wall_r.at[group, k],
                device_id={"wall": lax.rem(wall + k, WALL)}, device_id_type=MESH)
            copy.start()
            copies.append(copy)
        return copies

    lhs_copies = to_wall(lhs.at[wall], MODES)
    for j in range(len(PIECES)):
        there[1, j].start()

    def factor():
        for copy in lhs_copies:
            copy.wait_recv()
        for mode in range(MODES):
            ratio = zero
            for w in range(WALL):
                sep_up = row_of(seps, w)
                last = w == WALL - 1
                pivot = lhs[w, mode, 0] + (sep_up if last else sep_up * lhs[w + 1, mode, 2])
                link = lhs[w, mode, 1]
                inv = 1.0 / (pivot - link * ratio if w else pivot)
                ratio = zero if last else sep_up * lhs[w + 1, mode, 3] * inv
                sep[mode, w, 0] = inv
                sep[mode, w, 1] = link * inv if w else zero
                sep[mode, w, 2] = ratio

    for copy in own:
        copy.wait()
    own = []
    wall_copies = []
    for mode in range(MODES):
        for j in range(len(PIECES)):
            there[mode, j].wait_recv()

        def outer(i, carry):
            rows = pl.ds(pl.multiple_of(i * 8, 8), 8)
            block = [(land[mode, s, 0, rows, :], land[mode, s, 1, rows, :]) for s in range(SPAN)]
            for b, (re, im) in enumerate(sixteen(block, -1)):
                cos = jnp.broadcast_to(twist[0, b:b + 1, :], (8, CELLS))
                sin = jnp.broadcast_to(twist[1, b:b + 1, :], (8, CELLS))
                into = pl.ds(pl.multiple_of(b * ROWS + i * 8, 8), 8)
                grid[0, into, :] = re * cos + im * sin
                grid[1, into, :] = im * cos - re * sin
            return carry

        lax.fori_loop(0, ROWS // 8, outer, 0)

        def inner(i, carry):
            rows = pl.ds(pl.multiple_of(i * 512, 512), 512)
            both = product(jnp.concatenate([grid[0, rows, :], grid[1, rows, :]], axis=1), mats[0], mats[1])
            spec[0, rows, :] = both[:, :CELLS]
            spec[1, rows, :] = both[:, CELLS:]
            return carry

        lax.fori_loop(0, NZ // 512, inner, 0)

        def forward(i, state):
            prev = list(state)
            for k in range(UNROLL):
                row = i * UNROLL + k
                gain, carry = t_gain[mode, at(row), :], t_carry[mode, at(row), :]
                for c in range(2):
                    prev[c] = spec[c, pl.ds(row, SPAN, stride=ROWS), :] * gain + carry * prev[c]
                    vals[c, at(row), :] = prev[c]
            return tuple(prev)

        lax.fori_loop(0, ROWS // UNROLL, forward, (zero, zero))

        def backward(i, state):
            after = list(state)
            for k in range(UNROLL):
                row = LAST - (i * UNROLL + k)
                ratio = t_ratio[mode, at(row), :]
                for c in range(2):
                    after[c] = vals[c, at(row), :] + ratio * after[c]
                    vals[c, at(row), :] = after[c]
            return tuple(after)

        final = [vals[c, at(LAST - 1), :] for c in range(2)]
        first = lax.fori_loop(0, ROWS // UNROLL, backward, (zero, zero))
        for c in range(2):
            source = spec[c, pl.ds(LAST, SPAN, stride=ROWS), :] * (span_sq * wei_l)
            rhs[mode, wall, 0, c] = source + low_l * final[c]
            rhs[mode, wall, 1, c] = first[c]
        copies = to_wall(rhs.at[mode, wall], mode)
        wall_copies += copies
        if mode == 0:
            factor()
        else:
            for j in range(HELD, len(PIECES)):
                back[0, j].start()
        for copy in copies:
            copy.wait_recv()

        for c in range(2):
            value, values = None, []
            for w in range(WALL):
                r = rhs[mode, w, 0, c]
                if w < WALL - 1:
                    r = r + row_of(seps, w) * rhs[mode, w + 1, 1, c]
                value = r * sep[mode, w, 0] if w == 0 else r * sep[mode, w, 0] + sep[mode, w, 1] * value
                values.append(value)
            for w in range(WALL - 2, -1, -1):
                values[w] = values[w] + sep[mode, w, 2] * values[w + 1]
            for w in range(WALL):
                solved[w, c] = values[w]
        here = [solved[wall, c] for c in range(2)]
        up_at = lax.rem(wall + WALL - 1, WALL)
        there_is = (wall > 0).astype(F32)
        over = [solved[up_at, c] * there_is for c in range(2)]

        def inner_back(i, carry):
            rows = pl.ds(pl.multiple_of(i * 512, 512), 512)
            shape = (512 // SPAN, SPAN, CELLS)
            above = t_above[mode, rows, :].reshape(shape)
            below = t_below[mode, rows, :].reshape(shape)
            parts = [
                (vals[c, rows, :].reshape(shape) + above * over[c][None] + below * here[c][None]).reshape(512, CELLS)
                for c in range(2)]
            both = product(jnp.concatenate(parts, axis=1), mats[2], mats[3])
            re, im = both[:, :CELLS].reshape(shape), both[:, CELLS:].reshape(shape)
            cos, sin = twist[0][None], twist[1][None]
            grid[0, rows, :] = (re * cos - im * sin).reshape(512, CELLS)
            grid[1, rows, :] = (re * sin + im * cos).reshape(512, CELLS)
            return carry

        lax.fori_loop(0, NZ // 512, inner_back, 0)

        def outer_back(i, carry):
            block = [(grid[0, pl.ds(i * (8 * SPAN) + b, 8, stride=SPAN), :],
                      grid[1, pl.ds(i * (8 * SPAN) + b, 8, stride=SPAN), :]) for b in range(SPAN)]
            rows = pl.ds(pl.multiple_of(i * 8, 8), 8)
            for s, (re, im) in enumerate(sixteen(block, 1)):
                stage[mode, s, 0, rows, :] = re
                stage[mode, s, 1, rows, :] = im
            return carry

        lax.fori_loop(0, ROWS // 8, outer_back, 0)

        for m, j in GATES[mode]:
            there[m, j].wait_send()
        for j in range(HELD if mode == 0 else len(PIECES)):
            back[mode, j].start()
        copy = pltpu.make_async_copy(stage.at[mode, me], o_ref.at[:, MODES * me + mode], local.at[mode])
        copy.start()
        own.append(copy)

    for copy in lhs_copies + wall_copies:
        copy.wait_send()
    for mode in range(MODES):
        own[mode].wait()
        for j in range(len(PIECES)):
            back[mode, j].wait()


def solution(mesh):
    def body(stress):
        vmem = lambda *shape: pltpu.VMEM(shape, F32)
        dma = lambda *shape: pltpu.SemaphoreType.DMA(shape)
        table = (MODES, NZ * ROWS // CELLS, CELLS)
        return pl.pallas_call(
            kernel,
            out_shape=jax.ShapeDtypeStruct(stress.shape, F32),
            in_specs=[pl.BlockSpec(memory_space=pltpu.HBM)],
            out_specs=pl.BlockSpec(memory_space=pl.ANY),
            scratch_shapes=[
                vmem(MODES, SPAN, 2, ROWS, CELLS),
                vmem(MODES, SPAN, 2, ROWS, CELLS),
                vmem(2, SPAN * ROWS, CELLS),
                vmem(2, SPAN * ROWS, CELLS),
                vmem(2, SPAN * ROWS, CELLS),
                vmem(ROWS, 128), vmem(ROWS, 128), vmem(ROWS, 128),
                vmem(*table), vmem(*table), vmem(*table), vmem(*table), vmem(*table),
                vmem(WALL, MODES, 4, SPAN, CELLS),
                vmem(MODES, WALL, 3, SPAN, CELLS),
                vmem(MODES, WALL, 2, 2, SPAN, CELLS),
                vmem(WALL, 2, SPAN, CELLS),
                vmem(WALL, 128),
                pltpu.VMEM((4, 2 * CELLS, 2 * CELLS), BF16),
                vmem(2, SPAN, CELLS),
                dma(MODES, len(PIECES)), dma(MODES, len(PIECES)), dma(MODES, len(PIECES)), dma(MODES, len(PIECES)),
                dma(MODES + 1, WALL), dma(MODES + 1, WALL), dma(MODES),
            ],
            name="pressure",
            compiler_params=pltpu.CompilerParams(
                collective_id=1, has_side_effects=True, vmem_limit_bytes=48 << 20),
        )(stress)

    placed = P(None, None, "wall", "span")
    return jax.shard_map(body, mesh=mesh, in_specs=(placed,), out_specs=placed, check_vma=False)
```

```python
import math

import jax
import jax.numpy as jnp
from jax import lax
from jax.experimental import pallas as pl
from jax.experimental.pallas import tpu as pltpu
from jax.sharding import PartitionSpec as P

MESH = pl.DeviceIdType.MESH
F32 = jnp.float32
BF16 = jnp.bfloat16

NZ, NY, KX = 2048, 1024, 32
SPAN, WALL = 16, 8
ROWS = NY // WALL
CELLS = NZ // SPAN
MODES = KX // SPAN
LAST = ROWS - 1
STRETCH = 2.0
UNROLL = 8

OFFSETS = [(2, 2), (1, 1), (3, 3), (0, 2), (1, 3), (3, 1), (2, 0), (2, 1), (1, 2), (2, 3), (3, 2),
           (1, 0), (0, 1), (3, 0), (0, 3)]
PIECES = [(offset, part) for part in range(2) for offset in OFFSETS]
EARLY = [(0, j) for j in range(30)] + [(1, j) for j in range(15)]
HELD = 10
GATES = (EARLY, [(1, j) for j in range(15, 30)])


def times(value, cos, sin):
    re, im = value
    return re * cos - im * sin, re * sin + im * cos


def four(x, sign):
    (ar, ai), (br, bi), (cr, ci), (dr, di) = x
    er, ei, fr, fi = ar + cr, ai + ci, ar - cr, ai - ci
    gr, gi, hr, hi = br + dr, bi + di, br - dr, bi - di
    if sign > 0:
        return [(er + gr, ei + gi), (fr - hi, fi + hr), (er - gr, ei - gi), (fr + hi, fi - hr)]
    return [(er + gr, ei + gi), (fr + hi, fi - hr), (er - gr, ei - gi), (fr - hi, fi + hr)]


def sixteen(x, sign):
    half = math.sqrt(0.5)
    first = [four([x[4 * i + j] for i in range(4)], sign) for j in range(4)]
    out = [None] * 16
    for k in range(4):
        col = []
        for j in range(4):
            re, im = first[j][k]
            power = j * k
            if power == 0:
                col.append((re, im))
            elif power == 2:
                col.append(((re - sign * im) * half, (im + sign * re) * half))
            elif power == 4:
                col.append((-im, re) if sign > 0 else (im, -re))
            elif power == 6:
                col.append(((-re - sign * im) * half, (sign * re - im) * half))
            else:
                angle = 2.0 * math.pi * power / 16
                col.append(times((re, im), math.cos(angle), sign * math.sin(angle)))
        for p, value in enumerate(four(col, sign)):
            out[k + 4 * p] = value
    return out


def product(x, high, low):
    x_high = x.astype(BF16)
    x_low = (x - x_high.astype(F32)).astype(BF16)
    dot = lambda a, b: jnp.dot(a, b, preferred_element_type=F32)
    return dot(x_high, high) + (dot(x_low, high) + dot(x_high, low))


def kernel(x_ref, o_ref, land, stage, grid, spec, vals, low_s, upp_s, wei_s,
           t_gain, t_carry, t_ratio, t_above, t_below, lhs, sep, rhs, solved, seps, mats, twist,
           there_s, there_r, back_s, back_r, wall_s, wall_r, local):
    me = lax.axis_index("span")
    wall = lax.axis_index("wall")
    y, z = me // 4, me % 4

    def peer(offset):
        return lax.rem(y + offset[0], 4) * 4 + lax.rem(z + offset[1], 4)

    barrier = pltpu.get_barrier_semaphore()
    for offset in OFFSETS:
        pl.semaphore_signal(barrier, inc=1, device_id={"span": peer(offset)}, device_id_type=MESH)
    for k in range(1, WALL):
        pl.semaphore_signal(barrier, inc=1, device_id={"wall": lax.rem(wall + k, WALL)}, device_id_type=MESH)
    pl.semaphore_wait(barrier, SPAN - 1 + WALL - 1)

    there, back = {}, {}
    for mode in range(MODES):
        for j, (offset, part) in enumerate(PIECES):
            to = peer(offset)
            there[mode, j] = pltpu.make_async_remote_copy(
                src_ref=x_ref.at[part, MODES * to + mode], dst_ref=land.at[mode, me, part],
                send_sem=there_s.at[mode, j], recv_sem=there_r.at[mode, j],
                device_id={"span": to}, device_id_type=MESH)
            back[mode, j] = pltpu.make_async_remote_copy(
                src_ref=stage.at[mode, to, part], dst_ref=o_ref.at[part, MODES * me + mode],
                send_sem=back_s.at[mode, j], recv_sem=back_r.at[mode, j],
                device_id={"span": to}, device_id_type=MESH)
    for j in range(len(PIECES)):
        there[0, j].start()
    own = [pltpu.make_async_copy(x_ref.at[:, MODES * me + mode], land.at[mode, me], local.at[mode])
           for mode in range(MODES)]
    for copy in own:
        copy.start()

    def circle(rows, length):
        shape = (rows, CELLS)
        steps = lax.broadcasted_iota(jnp.int32, shape, 0) * lax.broadcasted_iota(jnp.int32, shape, 1)
        angle = lax.rem(steps, length).astype(F32) * F32(2.0 * math.pi / length)
        return jnp.cos(angle), jnp.sin(angle)

    twist[0], twist[1] = circle(SPAN, NZ)
    cos, sin = circle(CELLS, CELLS)
    for which, (re, im) in enumerate([(cos, -sin), (cos * F32(1 / NZ), sin * F32(1 / NZ))]):
        for r, c, value in [(0, 0, re), (0, 1, im), (1, 0, -im), (1, 1, re)]:
            high = value.astype(BF16)
            place = (pl.ds(r * CELLS, CELLS), pl.ds(c * CELLS, CELLS))
            mats[2 * which, *place] = high
            mats[2 * which + 1, *place] = (value - high.astype(F32)).astype(BF16)

    scale = math.sinh(2.0 * STRETCH / (NY + 1)) / math.tanh(STRETCH)

    def bands(cell):
        def cosh(k):
            xi = (2 * (cell + k) - (NY + 1)).astype(F32) * F32(STRETCH / (NY + 1))
            return 0.5 * (jnp.exp(xi) + jnp.exp(-xi))
        c0, c1, c2 = cosh(0), cosh(1), cosh(2)
        total = c0 + c2
        return c0 / total, c2 / total, (0.5 * scale * scale) / (c0 * c2 * (c1 * c1))

    cell = lax.broadcasted_iota(jnp.int32, (ROWS, 128), 0) + wall * ROWS
    low, upp, wei = bands(cell)
    low_s[...] = low
    upp_s[...] = upp
    wei_s[...] = wei
    sep_cell = lax.broadcasted_iota(jnp.int32, (WALL, 128), 0) * ROWS + LAST
    _, sep_upp, _ = bands(sep_cell)
    seps[...] = sep_upp

    freq = lax.broadcasted_iota(jnp.int32, (SPAN, CELLS), 1) * SPAN + lax.broadcasted_iota(jnp.int32, (SPAN, CELLS), 0)
    freq = jnp.where(freq >= NZ // 2, freq - NZ, freq)
    span_sq = jnp.square(freq.astype(F32) * F32(2.0 / 3.0))
    wave = [span_sq + jnp.square((me * MODES + mode).astype(F32) * F32(0.25)) for mode in range(MODES)]
    one = jnp.ones((SPAN, CELLS), F32)
    zero = jnp.zeros((SPAN, CELLS), F32)

    def at(row):
        return pl.ds(pl.multiple_of(row * SPAN, SPAN), SPAN)

    def row_of(ref, row):
        return jnp.broadcast_to(ref[pl.ds(row, 1), :], (SPAN, CELLS))

    def down(row, tops):
        low, upp, wei = row_of(low_s, row), row_of(upp_s, row), row_of(wei_s, row)
        new = []
        for mode in range(MODES):
            d = wave[mode] * wei + low * tops[mode]
            inv = 1.0 / (d + upp)
            t_gain[mode, at(row), :] = span_sq * (wei * inv)
            t_carry[mode, at(row), :] = low * inv
            t_ratio[mode, at(row), :] = upp * inv
            new.append(d * inv)
        return tuple(new)

    tops = lax.fori_loop(0, LAST, down, (one,) * MODES)
    low_l, wei_l = row_of(low_s, LAST), row_of(wei_s, LAST)
    for mode in range(MODES):
        lhs[wall, mode, 0] = wave[mode] * wei_l + low_l * tops[mode]
        t_gain[mode, at(LAST), :] = zero
        t_carry[mode, at(LAST), :] = zero
        t_ratio[mode, at(LAST), :] = zero
        t_above[mode, at(LAST), :] = zero
        t_below[mode, at(LAST), :] = one

    def up(i, state):
        row = LAST - 1 - i
        low, upp, wei = row_of(low_s, row), row_of(upp_s, row), row_of(wei_s, row)
        new = []
        for mode in range(MODES):
            under, below = state[mode]
            e = wave[mode] * wei + upp * under
            inv = 1.0 / (e + low)
            t_above[mode, at(row), :] = low * inv
            below = below * t_ratio[mode, at(row), :]
            t_below[mode, at(row), :] = below
            new.append((e * inv, below))
        return tuple(new)

    ends = lax.fori_loop(0, LAST, up, ((one, one),) * MODES)

    def across(row, state):
        new = []
        for mode in range(MODES):
            above = state[mode] * t_above[mode, at(row), :]
            t_above[mode, at(row), :] = above
            new.append(above)
        return tuple(new)

    above = lax.fori_loop(0, LAST, across, (one,) * MODES)
    for mode in range(MODES):
        lhs[wall, mode, 1] = low_l * above[mode]
        lhs[wall, mode, 2] = ends[mode][0]
        lhs[wall, mode, 3] = ends[mode][1]

    def to_wall(ref, group):
        copies = []
        for k in range(1, WALL):
            copy = pltpu.make_async_remote_copy(
                src_ref=ref, dst_ref=ref, send_sem=wall_s.at[group, k], recv_sem=wall_r.at[group, k],
                device_id={"wall": lax.rem(wall + k, WALL)}, device_id_type=MESH)
            copy.start()
            copies.append(copy)
        return copies

    lhs_copies = to_wall(lhs.at[wall], MODES)
    for j in range(len(PIECES)):
        there[1, j].start()

    def factor():
        for copy in lhs_copies:
            copy.wait_recv()
        for mode in range(MODES):
            ratio = zero
            for w in range(WALL):
                sep_up = row_of(seps, w)
                last = w == WALL - 1
                pivot = lhs[w, mode, 0] + (sep_up if last else sep_up * lhs[w + 1, mode, 2])
                link = lhs[w, mode, 1]
                inv = 1.0 / (pivot - link * ratio if w else pivot)
                ratio = zero if last else sep_up * lhs[w + 1, mode, 3] * inv
                sep[mode, w, 0] = inv
                sep[mode, w, 1] = link * inv if w else zero
                sep[mode, w, 2] = ratio

    for copy in own:
        copy.wait()
    own = []
    wall_copies = []
    for mode in range(MODES):
        for j in range(len(PIECES)):
            there[mode, j].wait_recv()

        def outer(i, carry):
            rows = pl.ds(pl.multiple_of(i * 8, 8), 8)
            block = [(land[mode, s, 0, rows, :], land[mode, s, 1, rows, :]) for s in range(SPAN)]
            for b, (re, im) in enumerate(sixteen(block, -1)):
                cos = jnp.broadcast_to(twist[0, b:b + 1, :], (8, CELLS))
                sin = jnp.broadcast_to(twist[1, b:b + 1, :], (8, CELLS))
                into = pl.ds(pl.multiple_of(b * ROWS + i * 8, 8), 8)
                grid[0, into, :] = re * cos + im * sin
                grid[1, into, :] = im * cos - re * sin
            return carry

        lax.fori_loop(0, ROWS // 8, outer, 0)

        def inner(i, carry):
            rows = pl.ds(pl.multiple_of(i * 512, 512), 512)
            both = product(jnp.concatenate([grid[0, rows, :], grid[1, rows, :]], axis=1), mats[0], mats[1])
            spec[0, rows, :] = both[:, :CELLS]
            spec[1, rows, :] = both[:, CELLS:]
            return carry

        lax.fori_loop(0, NZ // 512, inner, 0)

        def forward(i, state):
            prev = list(state)
            for k in range(UNROLL):
                row = i * UNROLL + k
                gain, carry = t_gain[mode, at(row), :], t_carry[mode, at(row), :]
                for c in range(2):
                    prev[c] = spec[c, pl.ds(row, SPAN, stride=ROWS), :] * gain + carry * prev[c]
                    vals[c, at(row), :] = prev[c]
            return tuple(prev)

        lax.fori_loop(0, ROWS // UNROLL, forward, (zero, zero))

        def backward(i, state):
            after = list(state)
            for k in range(UNROLL):
                row = LAST - (i * UNROLL + k)
                ratio = t_ratio[mode, at(row), :]
                for c in range(2):
                    after[c] = vals[c, at(row), :] + ratio * after[c]
                    vals[c, at(row), :] = after[c]
            return tuple(after)

        final = [vals[c, at(LAST - 1), :] for c in range(2)]
        first = lax.fori_loop(0, ROWS // UNROLL, backward, (zero, zero))
        for c in range(2):
            source = spec[c, pl.ds(LAST, SPAN, stride=ROWS), :] * (span_sq * wei_l)
            rhs[mode, wall, 0, c] = source + low_l * final[c]
            rhs[mode, wall, 1, c] = first[c]
        copies = to_wall(rhs.at[mode, wall], mode)
        wall_copies += copies
        if mode == 0:
            factor()
        else:
            for j in range(HELD, len(PIECES)):
                back[0, j].start()
        for copy in copies:
            copy.wait_recv()

        for c in range(2):
            value, values = None, []
            for w in range(WALL):
                r = rhs[mode, w, 0, c]
                if w < WALL - 1:
                    r = r + row_of(seps, w) * rhs[mode, w + 1, 1, c]
                value = r * sep[mode, w, 0] if w == 0 else r * sep[mode, w, 0] + sep[mode, w, 1] * value
                values.append(value)
            for w in range(WALL - 2, -1, -1):
                values[w] = values[w] + sep[mode, w, 2] * values[w + 1]
            for w in range(WALL):
                solved[w, c] = values[w]
        here = [solved[wall, c] for c in range(2)]
        up_at = lax.rem(wall + WALL - 1, WALL)
        there_is = (wall > 0).astype(F32)
        over = [solved[up_at, c] * there_is for c in range(2)]

        def inner_back(i, carry):
            rows = pl.ds(pl.multiple_of(i * 512, 512), 512)
            shape = (512 // SPAN, SPAN, CELLS)
            above = t_above[mode, rows, :].reshape(shape)
            below = t_below[mode, rows, :].reshape(shape)
            parts = [
                (vals[c, rows, :].reshape(shape) + above * over[c][None] + below * here[c][None]).reshape(512, CELLS)
                for c in range(2)]
            both = product(jnp.concatenate(parts, axis=1), mats[2], mats[3])
            re, im = both[:, :CELLS].reshape(shape), both[:, CELLS:].reshape(shape)
            cos, sin = twist[0][None], twist[1][None]
            grid[0, rows, :] = (re * cos - im * sin).reshape(512, CELLS)
            grid[1, rows, :] = (re * sin + im * cos).reshape(512, CELLS)
            return carry

        lax.fori_loop(0, NZ // 512, inner_back, 0)

        def outer_back(i, carry):
            block = [(grid[0, pl.ds(i * (8 * SPAN) + b, 8, stride=SPAN), :],
                      grid[1, pl.ds(i * (8 * SPAN) + b, 8, stride=SPAN), :]) for b in range(SPAN)]
            rows = pl.ds(pl.multiple_of(i * 8, 8), 8)
            for s, (re, im) in enumerate(sixteen(block, 1)):
                stage[mode, s, 0, rows, :] = re
                stage[mode, s, 1, rows, :] = im
            return carry

        lax.fori_loop(0, ROWS // 8, outer_back, 0)

        for m, j in GATES[mode]:
            there[m, j].wait_send()
        for j in range(HELD if mode == 0 else len(PIECES)):
            back[mode, j].start()
        copy = pltpu.make_async_copy(stage.at[mode, me], o_ref.at[:, MODES * me + mode], local.at[mode])
        copy.start()
        own.append(copy)

    for copy in lhs_copies + wall_copies:
        copy.wait_send()
    for mode in range(MODES):
        own[mode].wait()
        for j in range(len(PIECES)):
            back[mode, j].wait()


def solution(mesh):
    def body(stress):
        vmem = lambda *shape: pltpu.VMEM(shape, F32)
        dma = lambda *shape: pltpu.SemaphoreType.DMA(shape)
        table = (MODES, NZ * ROWS // CELLS, CELLS)
        return pl.pallas_call(
            kernel,
            out_shape=jax.ShapeDtypeStruct(stress.shape, F32),
            in_specs=[pl.BlockSpec(memory_space=pltpu.HBM)],
            out_specs=pl.BlockSpec(memory_space=pl.ANY),
            scratch_shapes=[
                vmem(MODES, SPAN, 2, ROWS, CELLS),
                vmem(MODES, SPAN, 2, ROWS, CELLS),
                vmem(2, SPAN * ROWS, CELLS),
                vmem(2, SPAN * ROWS, CELLS),
                vmem(2, SPAN * ROWS, CELLS),
                vmem(ROWS, 128), vmem(ROWS, 128), vmem(ROWS, 128),
                vmem(*table), vmem(*table), vmem(*table), vmem(*table), vmem(*table),
                vmem(WALL, MODES, 4, SPAN, CELLS),
                vmem(MODES, WALL, 3, SPAN, CELLS),
                vmem(MODES, WALL, 2, 2, SPAN, CELLS),
                vmem(WALL, 2, SPAN, CELLS),
                vmem(WALL, 128),
                pltpu.VMEM((4, 2 * CELLS, 2 * CELLS), BF16),
                vmem(2, SPAN, CELLS),
                dma(MODES, len(PIECES)), dma(MODES, len(PIECES)), dma(MODES, len(PIECES)), dma(MODES, len(PIECES)),
                dma(MODES + 1, WALL), dma(MODES + 1, WALL), dma(MODES),
            ],
            name="pressure",
            compiler_params=pltpu.CompilerParams(
                collective_id=1, has_side_effects=True, vmem_limit_bytes=48 << 20),
        )(stress)

    placed = P(None, None, "wall", "span")
    return jax.shard_map(body, mesh=mesh, in_specs=(placed,), out_specs=placed, check_vma=False)
```
